32 devices in a mesh: groups: 2 (over y), row: 2 (over x), col: 4 (over z), depth: 2 (over core).
Axes of the slice: x: 2, y: 2, z: 4, core: 2. Of those that a mesh axis runs over, the one named last changes fastest.
Arguments:
- layer_input: bfloat16 [4, 224, 4096], P(('groups', 'depth'), 'row', 'col'), parts along dimension 0, may hold values from -6 to 6
- out_grad: bfloat16 [4, 224, 4096], P(('groups', 'depth'), 'row', 'col'), parts along dimension 0, may hold values from -6 to 6
- gate_pre: bfloat16 [4, 224, 14336], P(('groups', 'depth'), 'col', 'row'), parts along dimension 0, may hold values from -6 to 6
- up_pre: bfloat16 [4, 224, 14336], P(('groups', 'depth'), 'col', 'row'), parts along dimension 0, may hold values from -6 to 6
- gate_weight: bfloat16 [4096, 14336], P('col', ('row', 'depth')), may hold values from -0.09375 to 0.09375
- up_weight: bfloat16 [4096, 14336], P('col', ('row', 'depth')), may hold values from -0.09375 to 0.09375
- down_weight: bfloat16 [14336, 4096], P(('row', 'depth'), 'col'), may hold values from -0.046875 to 0.046875
Outputs:
- input_grad: bfloat16 [4, 224, 4096], P(('groups', 'depth'), 'row', 'col'), parts along dimension 0
- gate_weight_grad: bfloat16 [4, 4096, 14336], P(('groups', 'depth'), 'col', 'row'), parts along dimension 0
- up_weight_grad: bfloat16 [4, 4096, 14336], P(('groups', 'depth'), 'col', 'row'), parts along dimension 0
- down_weight_grad: bfloat16 [4, 14336, 4096], P(('groups', 'depth'), 'row', 'col'), parts along dimension 0
The draws below stay inside these ranges and needn't reach their ends.
There are 2 independent parts, one for each index of `groups`. The reference program is written for one: setup_inputs(seed, part) draws one part's arguments, and reference() takes and returns one part's arrays. A program takes and returns all parts, laid end to end along the dimension named above; an argument that names none is the same for every part. Nothing has to cross between parts.
All inputs are finite; a program needn't handle non-finite values.
Results may differ from the reference program's by a relative error of at most 0.03.
Values may be sent and summed in bfloat16 or wider, within the bound.
A program may use at most 192 MiB of HBM per device.

```python
import jax
import jax.numpy as jnp

D = 4096
FF = 14336
SUBS = 2
SUBTOK = 224
N_ROW = 2
N_COL = 4


def with_spikes(drawn, own_key, source, target, parts, factor):
    owner, partner = [(jnp.arange(drawn.shape[axis_at]) // (drawn.shape[axis_at] // parts)).reshape([-1 if axis == axis_at else 1 for axis in range(drawn.ndim)]) for axis_at in (source, target)]
    chosen = jax.random.permutation(own_key, parts)[partner]
    strong = (owner == chosen) | (owner == (partner + parts // 2) % parts)
    return jnp.where(strong, factor * drawn, drawn)


def steps_of(key, shape, shards, smallest, high):
    gain = 1.0
    for axis_at, shards_of in shards:
        steps = jax.random.uniform(jax.random.fold_in(jax.random.fold_in(key, 6), axis_at), (shards_of,), jnp.float32, smallest / len(shards), high / len(shards))
        gain = gain * jnp.repeat(jnp.exp(steps), shape[axis_at] // shards_of).reshape((-1,) + (1,) * (len(shape) - 1 - axis_at))
    return gain


def gaussian(own_key, shape, scale, reach, shards=(), dtype=jnp.bfloat16):
    gain = steps_of(own_key, shape, shards, -0.22, 0.18) if shards else 1.0
    result = jax.random.normal(own_key, shape, jnp.float32) * scale * gain
    return jnp.minimum(jnp.maximum(result, -reach), reach).astype(dtype)


def bell_draw_with(own_key, dims, width, most, split, heavy, held_as=jnp.bfloat16):
    drawn = width * jax.random.normal(own_key, dims, jnp.float32)
    if split:
        drawn = drawn * steps_of(own_key, dims, split, -0.22, 0.18)
    return jnp.clip(with_spikes(drawn, jax.random.fold_in(own_key, 3), *heavy), -most, most).astype(held_as)


def setup_inputs(seed: int = 0, part: int = 0) -> dict:
    keys = jax.random.split(jax.random.key(seed), 8)
    own_keys = jax.random.split(jax.random.fold_in(keys[7], part), 8)
    layer_input = gaussian(own_keys[0], (SUBS, SUBTOK, D), 1.0, 6.0, ((0, 2), (1, 2), (2, 4)))
    out_grad = bell_draw_with(own_keys[1], (SUBS, SUBTOK, D), 1.0, 6.0, ((0, 2), (1, 2), (2, 4)), (2, 1, 4, 2.0))
    gate_pre = gaussian(own_keys[2], (SUBS, SUBTOK, FF), 1.0, 6.0, ((0, 2), (1, 4), (2, 2)))
    up_pre = gaussian(own_keys[3], (SUBS, SUBTOK, FF), 1.0, 6.0, ((0, 2), (1, 4), (2, 2)))
    gate_weight = gaussian(keys[4], (D, FF), D ** -0.5, 0.09375, ((0, 4), (1, 4)))
    up_weight = gaussian(keys[5], (D, FF), D ** -0.5, 0.09375, ((0, 4), (1, 4)))
    down_weight = gaussian(keys[6], (FF, D), FF ** -0.5, 0.046875, ((0, 4), (1, 4)))
    return {"layer_input": layer_input, "out_grad": out_grad, "gate_pre": gate_pre, "up_pre": up_pre, "gate_weight": gate_weight, "up_weight": up_weight, "down_weight": down_weight}


def swiglu_grads(hidden_grad, gate_rows, up_rows):
    gate_value = gate_rows.astype(jnp.float32)
    up_value = up_rows.astype(jnp.float32)
    sig = jax.nn.sigmoid(gate_value)
    silu_value = gate_value * sig
    hidden = (silu_value * up_value).astype(jnp.bfloat16)
    gate_grad = (hidden_grad * up_value * sig * (1.0 + gate_value * (1.0 - sig))).astype(jnp.bfloat16)
    up_grad = (hidden_grad * silu_value).astype(jnp.bfloat16)
    return gate_grad, up_grad, hidden


def reference(layer_input, out_grad, gate_pre, up_pre, gate_weight, up_weight, down_weight):
    input_list = []
    gate_list = []
    up_list = []
    down_list = []
    feat_block = D // N_COL
    unit_block = FF // N_ROW
    for sub_index in range(SUBS):
        input_rows = layer_input[sub_index]
        grad_rows = out_grad[sub_index]
        hidden_grad = jnp.zeros((SUBTOK, FF), jnp.float32)
        for block in range(N_COL):
            lo = block * feat_block
            partial_sum = jnp.dot(grad_rows[:, lo:lo + feat_block], down_weight[:, lo:lo + feat_block].T, preferred_element_type=jnp.float32)
            hidden_grad = hidden_grad + partial_sum.astype(jnp.bfloat16).astype(jnp.float32)
        gate_grad, up_grad, hidden = swiglu_grads(hidden_grad, gate_pre[sub_index], up_pre[sub_index])
        input_total = jnp.zeros((SUBTOK, D), jnp.float32)
        for block in range(N_ROW):
            lo = block * unit_block
            part_sum = jnp.dot(gate_grad[:, lo:lo + unit_block], gate_weight[:, lo:lo + unit_block].T, preferred_element_type=jnp.float32)
            part_sum = part_sum + jnp.dot(up_grad[:, lo:lo + unit_block], up_weight[:, lo:lo + unit_block].T, preferred_element_type=jnp.float32)
            input_total = input_total + part_sum.astype(jnp.bfloat16).astype(jnp.float32)
        input_list.append(input_total.astype(jnp.bfloat16))
        gate_list.append(jnp.dot(input_rows.T, gate_grad, preferred_element_type=jnp.float32).astype(jnp.bfloat16))
        up_list.append(jnp.dot(input_rows.T, up_grad, preferred_element_type=jnp.float32).astype(jnp.bfloat16))
        down_list.append(jnp.dot(hidden.T, grad_rows, preferred_element_type=jnp.float32).astype(jnp.bfloat16))
    return (jnp.stack(input_list), jnp.stack(gate_list), jnp.stack(up_list), jnp.stack(down_list))
```

```python
import functools

import jax
import jax.numpy as jnp
from jax import lax
from jax.experimental import pallas as pl
from jax.experimental.pallas import tpu as pltpu
from jax.sharding import PartitionSpec as P

MESH = pl.DeviceIdType.MESH
BF16 = jnp.bfloat16
F32 = jnp.float32


def dot_last(left, right):
    return lax.dot_general(
        left, right, (((1,), (1,)), ((), ())), preferred_element_type=F32
    )


def dot_first(left, right):
    return lax.dot_general(
        left, right, (((0,), (0,)), ((), ())), preferred_element_type=F32
    )


def exchange_kernel(
    n_row, n_col, n_chunk,
    x_in, og_in, g_in, u_in, gw_in, uw_in, dw_in,
    x_out, og_out, act_out, ig_out,
    og, gu, own, fin, bin_, fout, bout, res, acc, part, inbox, gw, uw, dw,
    og_send, og_recv, x_send, x_recv, dep_send, dep_recv, loc,
    gu_send, gu_recv, ar_send, ar_recv, res_send, res_recv, res_loc,
    ig_send, ig_recv, w_sem, dw_sem,
):
    row, col, dep = lax.axis_index("row"), lax.axis_index("col"), lax.axis_index("depth")
    other = 1 - dep
    toks = x_in.shape[1]
    small = g_in.shape[1]
    units = gw_in.shape[1]
    width = units // n_chunk
    me = dep * n_row + row
    n_peer = 2 * n_row
    has_next = col < n_col - 1
    has_prev = col > 0

    def peer(k):
        idx = lax.rem(me + k, n_peer)
        return idx, {"row": lax.rem(idx, n_row), "depth": idx // n_row}

    def next_prev(direction):
        if direction == 0:
            return has_prev, has_next, {"col": jnp.minimum(col + 1, n_col - 1)}
        return has_next, has_prev, {"col": jnp.maximum(col - 1, 0)}

    barrier = pltpu.get_barrier_semaphore()
    for k in range(1, n_peer):
        pl.semaphore_signal(barrier, inc=1, device_id=peer(k)[1], device_id_type=MESH)
    for direction in range(2):
        _, going, to = next_prev(direction)

        @pl.when(going)
        def _():
            pl.semaphore_signal(barrier, inc=1, device_id=to, device_id_type=MESH)

    load_gw = pltpu.make_async_copy(gw_in, gw, w_sem.at[0])
    load_uw = pltpu.make_async_copy(uw_in, uw, w_sem.at[1])

    def load_dw(i):
        slot = lax.rem(i, 2)
        return pltpu.make_async_copy(
            dw_in.at[pl.ds(i * width, width)], dw.at[slot], dw_sem.at[slot]
        )

    load_dw(0).start()
    own_g = [
        pltpu.make_async_copy(
            src.at[0, :, pl.ds(pl.multiple_of(dep * units, 128), units)],
            gu.at[a, col, dep], loc.at[a],
        )
        for a, src in enumerate((g_in, u_in))
    ]
    for copy in own_g:
        copy.start()
    own_og = pltpu.make_async_copy(og_in.at[0], og.at[me], loc.at[2])
    own_og.start()
    own_x = pltpu.make_async_copy(x_in.at[0], x_out.at[row], loc.at[3])
    own_x.start()

    beside = jnp.where(has_next, 1, 0) + jnp.where(has_prev, 1, 0)
    pl.semaphore_wait(barrier, n_peer - 1 + beside)

    dep_copies = [
        pltpu.make_async_remote_copy(
            src_ref=src.at[0, :, pl.ds(pl.multiple_of(other * units, 128), units)],
            dst_ref=gu.at[a, col, dep],
            send_sem=dep_send.at[a], recv_sem=dep_recv.at[a],
            device_id={"depth": other}, device_id_type=MESH,
        )
        for a, src in enumerate((g_in, u_in))
    ]

    def arrived(a):
        return pltpu.make_async_remote_copy(
            src_ref=gu.at[a, col, other], dst_ref=gu.at[a, col, other],
            send_sem=dep_send.at[a], recv_sem=dep_recv.at[a],
            device_id={"depth": other}, device_id_type=MESH,
        )

    def og_copy(k):
        idx, to = peer(k)
        return pltpu.make_async_remote_copy(
            src_ref=og_in.at[0], dst_ref=og.at[me],
            send_sem=og_send.at[k], recv_sem=og_recv.at[me],
            device_id=to, device_id_type=MESH,
        )

    def og_from(k):
        idx, to = peer(k)
        return pltpu.make_async_remote_copy(
            src_ref=og.at[idx], dst_ref=og.at[idx],
            send_sem=og_send.at[k], recv_sem=og_recv.at[idx],
            device_id=to, device_id_type=MESH,
        )

    def x_copy(k):
        idx = lax.rem(row + k, n_row)
        return pltpu.make_async_remote_copy(
            src_ref=x_in.at[0], dst_ref=x_out.at[row],
            send_sem=x_send.at[k], recv_sem=x_recv.at[row],
            device_id={"row": idx}, device_id_type=MESH,
        )

    def x_from(k):
        idx = lax.rem(row + k, n_row)
        return pltpu.make_async_remote_copy(
            src_ref=x_out.at[idx], dst_ref=x_out.at[idx],
            send_sem=x_send.at[k], recv_sem=x_recv.at[idx],
            device_id={"row": idx}, device_id_type=MESH,
        )

    def gu_copy(direction, block, a, s):
        to = next_prev(direction)[2]
        m = 2 * a + s
        return pltpu.make_async_remote_copy(
            src_ref=gu.at[a, block, s], dst_ref=gu.at[a, block, s],
            send_sem=gu_send.at[direction, block, m],
            recv_sem=gu_recv.at[direction, block, m],
            device_id=to, device_id_type=MESH,
        )

    for copy in dep_copies:
        copy.start()
    for k in range(1, n_peer):
        og_copy(k).start()
    for copy in own_g:
        copy.wait()
    for a in range(2):
        for direction in range(2):
            @pl.when(next_prev(direction)[1])
            def _():
                gu_copy(direction, col, a, dep).start()
    for a in range(2):
        arrived(a).wait_recv()
        for direction in range(2):
            @pl.when(next_prev(direction)[1])
            def _():
                gu_copy(direction, col, a, other).start()
    for k in range(1, n_row):
        x_copy(k).start()
    load_gw.start()
    load_uw.start()

    own_og.wait()
    for k in range(1, n_peer):
        og_from(k).wait_recv()
    keep_og = pltpu.make_async_copy(og.at[pl.ds(dep * n_row, n_row)], og_out, loc.at[4])
    keep_og.start()

    def partial(i, _):
        load_dw(i).wait()

        @pl.when(i + 1 < n_chunk)
        def _():
            load_dw(i + 1).start()
        rows = og[...].reshape(n_peer * toks, og.shape[2])
        product = dot_last(rows, dw[lax.rem(i, 2)])
        own[i] = product.reshape(2 * n_col, small, width).astype(BF16)
        return 0

    lax.fori_loop(0, n_chunk, partial, 0)

    def gu_step(step):
        for m in range(4):
            a, s = m % 2, m // 2
            for direction in range(2):
                coming, going, _ = next_prev(direction)
                block = col - 1 - step if direction == 0 else col + 1 + step
                valid = (block >= 0) & (block < n_col)
                half = dep if s == 0 else other

                @pl.when(valid)
                def _():
                    gu_copy(direction, block, a, half).wait_recv()

                    @pl.when(going)
                    def _():
                        gu_copy(direction, block, a, half).start()

    def gu_sent(step):
        for m in range(4):
            for direction in range(2):
                _, going, _ = next_prev(direction)
                block = col - step if direction == 0 else col + step
                valid = (block >= 0) & (block < n_col)

                @pl.when(valid & going)
                def _():
                    gu_copy(direction, block, m // 2, m % 2).wait_send()

    def ar_copy(direction, i, src):
        dst = fin if direction == 0 else bin_
        return pltpu.make_async_remote_copy(
            src_ref=src.at[i], dst_ref=dst.at[i],
            send_sem=ar_send.at[direction, i], recv_sem=ar_recv.at[direction, i],
            device_id=next_prev(direction)[2], device_id_type=MESH,
        )

    gu_step(0)
    gu_sent(0)
    for direction in range(2):
        coming, going, _ = next_prev(direction)

        @pl.when(jnp.logical_not(coming))
        def _():
            def first(i, _):
                ar_copy(direction, i, own).start()
                return 0
            lax.fori_loop(0, n_chunk, first, 0)
            land = fin if direction == 0 else bin_

            def clear(i, _):
                land[i] = jnp.zeros(land.shape[1:], BF16)
                return 0
            lax.fori_loop(0, n_chunk, clear, 0)

    if n_col > 2:
        def later(step, _):
            gu_step(step)
            return 0
        lax.fori_loop(1, n_col - 1, later, 0)

    load_gw.wait()
    load_uw.wait()
    acc[...] = jnp.zeros_like(acc)
    half_col = n_col // 2

    def res_copy(i):
        at = pl.multiple_of(dep * units + i * width, 128)
        return pltpu.make_async_remote_copy(
            src_ref=res.at[i, other], dst_ref=act_out.at[:, :, pl.ds(at, width)],
            send_sem=res_send.at[i], recv_sem=res_recv.at[i],
            device_id={"depth": other}, device_id_type=MESH,
        )

    def res_from(i):
        at = pl.multiple_of(other * units + i * width, 128)
        there = act_out.at[:, :, pl.ds(at, width)]
        return pltpu.make_async_remote_copy(
            src_ref=there, dst_ref=there,
            send_sem=res_send.at[i], recv_sem=res_recv.at[i],
            device_id={"depth": other}, device_id_type=MESH,
        )

    def res_keep(i):
        at = pl.multiple_of(dep * units + i * width, 128)
        return pltpu.make_async_copy(
            res.at[i, dep], act_out.at[:, :, pl.ds(at, width)], res_loc.at[i]
        )

    def slot(t, _):
        for direction in range(2):
            coming, going, _ = next_prev(direction)
            hops = col if direction == 0 else n_col - 1 - col
            i = t - hops
            land, leave = ((fin, fout), (bin_, bout))[direction]

            @pl.when(coming & (i >= 0) & (i < n_chunk))
            def _():
                ar_copy(direction, i, leave).wait_recv()

                @pl.when(going)
                def _():
                    leave[i] = (land[i].astype(F32) + own[i].astype(F32)).astype(BF16)
                    ar_copy(direction, i, leave).start()

        i = t - jnp.maximum(col, n_col - 1 - col)

        @pl.when((i >= 0) & (i < n_chunk))
        def _():
            cols = pl.ds(pl.multiple_of(i * width, 128), width)
            for s in range(2):
                def pair(p, _):
                    blocks = pl.ds(s * n_col + 2 * p, 2)
                    pair_at = pl.ds(2 * p, 2)
                    shape = (2 * small, width)
                    hg = (
                        fin[i, blocks].astype(F32) + own[i, blocks].astype(F32)
                        + bin_[i, blocks].astype(F32)
                    ).reshape(shape)
                    gate = gu[0, pair_at, s, :, cols].astype(F32).reshape(shape)
                    up = gu[1, pair_at, s, :, cols].astype(F32).reshape(shape)
                    sig = 1.0 / (1.0 + jnp.exp(-gate))
                    silu = gate * sig
                    at = pl.ds(pl.multiple_of(p * 2 * small, 16), 2 * small)
                    res[i, s, 0, at] = (hg * up * sig * (1.0 + gate * (1.0 - sig))).astype(BF16)
                    res[i, s, 1, at] = (hg * silu).astype(BF16)
                    res[i, s, 2, at] = (silu * up).astype(BF16)
                    return 0
                lax.fori_loop(0, half_col, pair, 0)
            res_copy(i).start()
            res_keep(i).start()
            for s in range(2):
                acc[s] += dot_last(res[i, s, 0], gw[:, cols]) + dot_last(res[i, s, 1], uw[:, cols])
        return 0

    lax.fori_loop(0, n_chunk + n_col - 1, slot, 0)

    part[...] = acc[...].reshape(part.shape).astype(BF16)

    def ig_copy(k):
        idx, to = peer(k)
        return pltpu.make_async_remote_copy(
            src_ref=part.at[idx], dst_ref=inbox.at[me],
            send_sem=ig_send.at[k], recv_sem=ig_recv.at[me],
            device_id=to, device_id_type=MESH,
        )

    def ig_from(k):
        idx, to = peer(k)
        return pltpu.make_async_remote_copy(
            src_ref=part.at[idx], dst_ref=inbox.at[idx],
            send_sem=ig_send.at[k], recv_sem=ig_recv.at[idx],
            device_id=to, device_id_type=MESH,
        )

    for k in range(1, n_peer):
        ig_copy(k).start()

    def finish(i, _):
        res_from(i).wait_recv()
        res_copy(i).wait_send()
        res_keep(i).wait()
        for direction in range(2):
            @pl.when(next_prev(direction)[1])
            def _():
                ar_copy(direction, i, own).wait_send()
        return 0

    lax.fori_loop(0, n_chunk, finish, 0)
    if n_col > 1:
        def sent(step, _):
            gu_sent(step)
            return 0
        lax.fori_loop(1, n_col - 1, sent, 0)
    for copy in dep_copies:
        copy.wait_send()
    own_x.wait()
    keep_og.wait()
    for k in range(1, n_row):
        x_copy(k).wait_send()
        x_from(k).wait_recv()
    total = part[me].astype(F32)
    for k in range(1, n_peer):
        og_copy(k).wait_send()
        ig_from(k).wait_recv()
        total += inbox[peer(k)[0]].astype(F32)
    ig_out[0] = total.astype(BF16)
    for k in range(1, n_peer):
        ig_copy(k).wait_send()


def exchange(n_row, n_col, x, og, g, u, gw, uw, dw):
    toks, feats = x.shape[1:]
    small = g.shape[1]
    units = gw.shape[1]
    n_chunk = 14 if units % (14 * 128) == 0 else 7
    width = units // n_chunk
    n_peer = 2 * n_row
    subtok = toks * n_row
    anywhere = pl.BlockSpec(memory_space=pl.ANY)
    line = pltpu.VMEM((n_chunk, 2 * n_col, small, width), BF16)
    dma = pltpu.SemaphoreType.DMA
    return pl.pallas_call(
        functools.partial(exchange_kernel, n_row, n_col, n_chunk),
        out_shape=(
            jax.ShapeDtypeStruct((n_row, toks, feats), BF16),
            jax.ShapeDtypeStruct((n_row, toks, feats), BF16),
            jax.ShapeDtypeStruct((3, subtok, 2 * units), BF16),
            jax.ShapeDtypeStruct((1, toks, feats), BF16),
        ),
        in_specs=[anywhere] * 7,
        out_specs=(anywhere, anywhere, anywhere, pl.BlockSpec(memory_space=pltpu.VMEM)),
        scratch_shapes=[
            pltpu.VMEM((n_peer, toks, feats), BF16),
            pltpu.VMEM((2, n_col, 2, small, units), BF16),
            line, line, line, line, line,
            pltpu.VMEM((n_chunk, 2, 3, subtok, width), BF16),
            pltpu.VMEM((2, subtok, feats), F32),
            pltpu.VMEM((n_peer, toks, feats), BF16),
            pltpu.VMEM((n_peer, toks, feats), BF16),
            pltpu.VMEM((feats, units), BF16),
            pltpu.VMEM((feats, units), BF16),
            pltpu.VMEM((2, width, feats), BF16),
            dma((n_peer,)), dma((n_peer,)), dma((n_row,)), dma((n_row,)),
            dma((2,)), dma((2,)), dma((5,)),
            dma((2, n_col, 4)), dma((2, n_col, 4)),
            dma((2, n_chunk)), dma((2, n_chunk)),
            dma((n_chunk,)), dma((n_chunk,)), dma((n_chunk,)),
            dma((n_peer,)), dma((n_peer,)), dma((2,)), dma((2,)),
        ],
        compiler_params=pltpu.CompilerParams(
            collective_id=0, has_side_effects=True, vmem_limit_bytes=63 * 2**20
        ),
        name="exchange",
    )(x, og, g, u, gw, uw, dw)


def weight_grad_kernel(x_ref, og_ref, act_ref, gate_ref, up_ref, down_ref):
    x = x_ref[...]
    gate_ref[0] = dot_first(x, act_ref[0]).astype(BF16)
    up_ref[0] = dot_first(x, act_ref[1]).astype(BF16)
    down_ref[0] = dot_first(act_ref[2], og_ref[...]).astype(BF16)


def weight_grads(x, og, act):
    subtok, feats = x.shape
    units = act.shape[2]
    tile = 512 if units % 512 == 0 else 256
    whole = pl.BlockSpec((subtok, feats), lambda i: (0, 0))
    wide = pl.BlockSpec((1, feats, tile), lambda i: (0, 0, i))
    return pl.pallas_call(
        weight_grad_kernel,
        grid=(units // tile,),
        out_shape=(
            jax.ShapeDtypeStruct((1, feats, units), BF16),
            jax.ShapeDtypeStruct((1, feats, units), BF16),
            jax.ShapeDtypeStruct((1, units, feats), BF16),
        ),
        in_specs=[whole, whole, pl.BlockSpec((3, subtok, tile), lambda i: (0, 0, i))],
        out_specs=(wide, wide, pl.BlockSpec((1, tile, feats), lambda i: (0, i, 0))),
        compiler_params=pltpu.CompilerParams(vmem_limit_bytes=40 * 2**20),
        name="weight_grads",
    )(x, og, act)


def solution(mesh):
    n_row, n_col = mesh.shape["row"], mesh.shape["col"]

    def shards(x, og, g, u, gw, uw, dw):
        x_all, og_all, act, ig = exchange(n_row, n_col, x, og, g, u, gw, uw, dw)
        feats = x.shape[2]
        return (ig, *weight_grads(x_all.reshape(-1, feats), og_all.reshape(-1, feats), act))

    return jax.shard_map(
        shards,
        mesh=mesh,
        in_specs=(
            P(("groups", "depth"), "row", "col"),
            P(("groups", "depth"), "row", "col"),
            P(("groups", "depth"), "col", "row"),
            P(("groups", "depth"), "col", "row"),
            P("col", ("row", "depth")),
            P("col", ("row", "depth")),
            P(("row", "depth"), "col"),
        ),
        out_specs=(
            P(("groups", "depth"), "row", "col"),
            P(("groups", "depth"), "col", "row"),
            P(("groups", "depth"), "col", "row"),
            P(("groups", "depth"), "row", "col"),
        ),
        check_vma=False,
    )
```

```python
import functools

import jax
import jax.numpy as jnp
from jax import lax
from jax.experimental import pallas as pl
from jax.experimental.pallas import tpu as pltpu
from jax.sharding import PartitionSpec as P

MESH = pl.DeviceIdType.MESH
BF16 = jnp.bfloat16
F32 = jnp.float32


def dot_last(left, right):
    return lax.dot_general(
        left, right, (((1,), (1,)), ((), ())), preferred_element_type=F32
    )


def dot_first(left, right):
    return lax.dot_general(
        left, right, (((0,), (0,)), ((), ())), preferred_element_type=F32
    )


def exchange_kernel(
    n_row, n_col, n_chunk,
    x_in, og_in, g_in, u_in, gw_in, uw_in, dw_in,
    x_out, og_out, act_out, *rest,
):
    shares = rest[: 2 * n_row]
    (
        og, gu, own, fin, bin_, fout, bout, res, acc, gw, uw, dw,
        og_send, og_recv, x_send, x_recv, dep_send, dep_recv, loc,
        gu_send, gu_recv, ar_send, ar_recv, res_send, res_recv, res_loc,
        w_sem, dw_sem,
    ) = rest[2 * n_row :]
    row, col, dep = lax.axis_index("row"), lax.axis_index("col"), lax.axis_index("depth")
    other = 1 - dep
    toks = x_in.shape[1]
    small = g_in.shape[1]
    units = gw_in.shape[1]
    width = units // n_chunk
    me = dep * n_row + row
    n_peer = 2 * n_row
    has_next = col < n_col - 1
    has_prev = col > 0

    def peer(k):
        idx = lax.rem(me + k, n_peer)
        return idx, {"row": lax.rem(idx, n_row), "depth": idx // n_row}

    def next_prev(direction):
        if direction == 0:
            return has_prev, has_next, {"col": jnp.minimum(col + 1, n_col - 1)}
        return has_next, has_prev, {"col": jnp.maximum(col - 1, 0)}

    barrier = pltpu.get_barrier_semaphore()
    for k in range(1, n_peer):
        pl.semaphore_signal(barrier, inc=1, device_id=peer(k)[1], device_id_type=MESH)
    for direction in range(2):
        _, going, to = next_prev(direction)

        @pl.when(going)
        def _():
            pl.semaphore_signal(barrier, inc=1, device_id=to, device_id_type=MESH)

    load_gw = pltpu.make_async_copy(gw_in, gw, w_sem.at[0])
    load_uw = pltpu.make_async_copy(uw_in, uw, w_sem.at[1])

    def load_dw(i):
        slot = lax.rem(i, 2)
        return pltpu.make_async_copy(
            dw_in.at[pl.ds(i * width, width)], dw.at[slot], dw_sem.at[slot]
        )

    load_dw(0).start()
    own_g = [
        pltpu.make_async_copy(
            src.at[0, :, pl.ds(pl.multiple_of(dep * units, 128), units)],
            gu.at[a, col, dep], loc.at[a],
        )
        for a, src in enumerate((g_in, u_in))
    ]
    for copy in own_g:
        copy.start()
    own_og = pltpu.make_async_copy(og_in.at[0], og.at[me], loc.at[2])
    own_og.start()
    own_x = pltpu.make_async_copy(x_in.at[0], x_out.at[row], loc.at[3])
    own_x.start()

    beside = jnp.where(has_next, 1, 0) + jnp.where(has_prev, 1, 0)
    pl.semaphore_wait(barrier, n_peer - 1 + beside)

    dep_copies = [
        pltpu.make_async_remote_copy(
            src_ref=src.at[0, :, pl.ds(pl.multiple_of(other * units, 128), units)],
            dst_ref=gu.at[a, col, dep],
            send_sem=dep_send.at[a], recv_sem=dep_recv.at[a],
            device_id={"depth": other}, device_id_type=MESH,
        )
        for a, src in enumerate((g_in, u_in))
    ]

    def arrived(a):
        return pltpu.make_async_remote_copy(
            src_ref=gu.at[a, col, other], dst_ref=gu.at[a, col, other],
            send_sem=dep_send.at[a], recv_sem=dep_recv.at[a],
            device_id={"depth": other}, device_id_type=MESH,
        )

    def og_copy(k):
        idx, to = peer(k)
        return pltpu.make_async_remote_copy(
            src_ref=og_in.at[0], dst_ref=og.at[me],
            send_sem=og_send.at[k], recv_sem=og_recv.at[me],
            device_id=to, device_id_type=MESH,
        )

    def og_from(k):
        idx, to = peer(k)
        return pltpu.make_async_remote_copy(
            src_ref=og.at[idx], dst_ref=og.at[idx],
            send_sem=og_send.at[k], recv_sem=og_recv.at[idx],
            device_id=to, device_id_type=MESH,
        )

    def x_copy(k):
        idx = lax.rem(row + k, n_row)
        return pltpu.make_async_remote_copy(
            src_ref=x_in.at[0], dst_ref=x_out.at[row],
            send_sem=x_send.at[k], recv_sem=x_recv.at[row],
            device_id={"row": idx}, device_id_type=MESH,
        )

    def x_from(k):
        idx = lax.rem(row + k, n_row)
        return pltpu.make_async_remote_copy(
            src_ref=x_out.at[idx], dst_ref=x_out.at[idx],
            send_sem=x_send.at[k], recv_sem=x_recv.at[idx],
            device_id={"row": idx}, device_id_type=MESH,
        )

    def gu_copy(direction, block, a, s):
        to = next_prev(direction)[2]
        m = 2 * a + s
        return pltpu.make_async_remote_copy(
            src_ref=gu.at[a, block, s], dst_ref=gu.at[a, block, s],
            send_sem=gu_send.at[direction, block, m],
            recv_sem=gu_recv.at[direction, block, m],
            device_id=to, device_id_type=MESH,
        )

    for copy in dep_copies:
        copy.start()
    for k in range(1, n_peer):
        og_copy(k).start()
    for copy in own_g:
        copy.wait()
    for a in range(2):
        for direction in range(2):
            @pl.when(next_prev(direction)[1])
            def _():
                gu_copy(direction, col, a, dep).start()
    for a in range(2):
        arrived(a).wait_recv()
        for direction in range(2):
            @pl.when(next_prev(direction)[1])
            def _():
                gu_copy(direction, col, a, other).start()
    for k in range(1, n_row):
        x_copy(k).start()
    load_gw.start()
    load_uw.start()

    own_og.wait()
    for k in range(1, n_peer):
        og_from(k).wait_recv()
    keep_og = pltpu.make_async_copy(og.at[pl.ds(dep * n_row, n_row)], og_out, loc.at[4])
    keep_og.start()

    def partial(i, _):
        load_dw(i).wait()

        @pl.when(i + 1 < n_chunk)
        def _():
            load_dw(i + 1).start()
        rows = og[...].reshape(n_peer * toks, og.shape[2])
        product = dot_last(rows, dw[lax.rem(i, 2)])
        own[i] = product.reshape(2 * n_col, small, width).astype(BF16)
        return 0

    lax.fori_loop(0, n_chunk, partial, 0)

    def gu_step(step):
        for m in range(4):
            a, s = m % 2, m // 2
            for direction in range(2):
                coming, going, _ = next_prev(direction)
                block = col - 1 - step if direction == 0 else col + 1 + step
                valid = (block >= 0) & (block < n_col)
                half = dep if s == 0 else other

                @pl.when(valid)
                def _():
                    gu_copy(direction, block, a, half).wait_recv()

                    @pl.when(going)
                    def _():
                        gu_copy(direction, block, a, half).start()

    def gu_sent(step):
        for m in range(4):
            for direction in range(2):
                _, going, _ = next_prev(direction)
                block = col - step if direction == 0 else col + step
                valid = (block >= 0) & (block < n_col)

                @pl.when(valid & going)
                def _():
                    gu_copy(direction, block, m // 2, m % 2).wait_send()

    def ar_copy(direction, i, src):
        dst = fin if direction == 0 else bin_
        return pltpu.make_async_remote_copy(
            src_ref=src.at[i], dst_ref=dst.at[i],
            send_sem=ar_send.at[direction, i], recv_sem=ar_recv.at[direction, i],
            device_id=next_prev(direction)[2], device_id_type=MESH,
        )

    gu_step(0)
    gu_sent(0)
    for direction in range(2):
        coming, going, _ = next_prev(direction)

        @pl.when(jnp.logical_not(coming))
        def _():
            def first(i, _):
                ar_copy(direction, i, own).start()
                return 0
            lax.fori_loop(0, n_chunk, first, 0)
            land = fin if direction == 0 else bin_

            def clear(i, _):
                land[i] = jnp.zeros(land.shape[1:], BF16)
                return 0
            lax.fori_loop(0, n_chunk, clear, 0)

    if n_col > 2:
        def later(step, _):
            gu_step(step)
            return 0
        lax.fori_loop(1, n_col - 1, later, 0)

    load_gw.wait()
    load_uw.wait()
    acc[...] = jnp.zeros_like(acc)
    half_col = n_col // 2

    def res_copy(i):
        at = pl.multiple_of(dep * units + i * width, 128)
        return pltpu.make_async_remote_copy(
            src_ref=res.at[i, other], dst_ref=act_out.at[:, :, pl.ds(at, width)],
            send_sem=res_send.at[i], recv_sem=res_recv.at[i],
            device_id={"depth": other}, device_id_type=MESH,
        )

    def res_from(i):
        at = pl.multiple_of(other * units + i * width, 128)
        there = act_out.at[:, :, pl.ds(at, width)]
        return pltpu.make_async_remote_copy(
            src_ref=there, dst_ref=there,
            send_sem=res_send.at[i], recv_sem=res_recv.at[i],
            device_id={"depth": other}, device_id_type=MESH,
        )

    def res_keep(i):
        at = pl.multiple_of(dep * units + i * width, 128)
        return pltpu.make_async_copy(
            res.at[i, dep], act_out.at[:, :, pl.ds(at, width)], res_loc.at[i]
        )

    def slot(t, _):
        for direction in range(2):
            coming, going, _ = next_prev(direction)
            hops = col if direction == 0 else n_col - 1 - col
            i = t - hops
            land, leave = ((fin, fout), (bin_, bout))[direction]

            @pl.when(coming & (i >= 0) & (i < n_chunk))
            def _():
                ar_copy(direction, i, leave).wait_recv()

                @pl.when(going)
                def _():
                    leave[i] = (land[i].astype(F32) + own[i].astype(F32)).astype(BF16)
                    ar_copy(direction, i, leave).start()

        i = t - jnp.maximum(col, n_col - 1 - col)

        @pl.when((i >= 0) & (i < n_chunk))
        def _():
            cols = pl.ds(pl.multiple_of(i * width, 128), width)
            for s in range(2):
                def pair(p, _):
                    blocks = pl.ds(s * n_col + 2 * p, 2)
                    pair_at = pl.ds(2 * p, 2)
                    shape = (2 * small, width)
                    hg = (
                        fin[i, blocks].astype(F32) + own[i, blocks].astype(F32)
                        + bin_[i, blocks].astype(F32)
                    ).reshape(shape)
                    gate = gu[0, pair_at, s, :, cols].astype(F32).reshape(shape)
                    up = gu[1, pair_at, s, :, cols].astype(F32).reshape(shape)
                    sig = 1.0 / (1.0 + jnp.exp(-gate))
                    silu = gate * sig
                    at = pl.ds(pl.multiple_of(p * 2 * small, 16), 2 * small)
                    res[i, s, 0, at] = (hg * up * sig * (1.0 + gate * (1.0 - sig))).astype(BF16)
                    res[i, s, 1, at] = (hg * silu).astype(BF16)
                    res[i, s, 2, at] = (silu * up).astype(BF16)
                    return 0
                lax.fori_loop(0, half_col, pair, 0)
            res_copy(i).start()
            res_keep(i).start()
            for s in range(2):
                of_sub = pl.ds(s * n_row, n_row)
                acc[of_sub] += (
                    dot_last(res[i, s, 0], gw[:, cols]) + dot_last(res[i, s, 1], uw[:, cols])
                ).reshape(n_row, toks, acc.shape[2])
        return 0

    lax.fori_loop(0, n_chunk + n_col - 1, slot, 0)

    for k in range(n_peer):
        shares[k][...] = acc[peer(k)[0]].astype(BF16)

    def finish(i, _):
        res_from(i).wait_recv()
        res_copy(i).wait_send()
        res_keep(i).wait()
        for direction in range(2):
            @pl.when(next_prev(direction)[1])
            def _():
                ar_copy(direction, i, own).wait_send()
        return 0

    lax.fori_loop(0, n_chunk, finish, 0)
    if n_col > 1:
        def sent(step, _):
            gu_sent(step)
            return 0
        lax.fori_loop(1, n_col - 1, sent, 0)
    for copy in dep_copies:
        copy.wait_send()
    own_x.wait()
    keep_og.wait()
    for k in range(1, n_row):
        x_copy(k).wait_send()
        x_from(k).wait_recv()
    for k in range(1, n_peer):
        og_copy(k).wait_send()


def exchange(n_row, n_col, x, og, g, u, gw, uw, dw):
    toks, feats = x.shape[1:]
    small = g.shape[1]
    units = gw.shape[1]
    n_chunk = 14 if units % (14 * 128) == 0 else 7
    width = units // n_chunk
    n_peer = 2 * n_row
    subtok = toks * n_row
    anywhere = pl.BlockSpec(memory_space=pl.ANY)
    line = pltpu.VMEM((n_chunk, 2 * n_col, small, width), BF16)
    dma = pltpu.SemaphoreType.DMA
    return pl.pallas_call(
        functools.partial(exchange_kernel, n_row, n_col, n_chunk),
        out_shape=(
            jax.ShapeDtypeStruct((n_row, toks, feats), BF16),
            jax.ShapeDtypeStruct((n_row, toks, feats), BF16),
            jax.ShapeDtypeStruct((3, subtok, 2 * units), BF16),
            *[jax.ShapeDtypeStruct((toks, feats), BF16)] * n_peer,
        ),
        in_specs=[anywhere] * 7,
        out_specs=(anywhere, anywhere, anywhere, *[pl.BlockSpec(memory_space=pltpu.VMEM)] * n_peer),
        scratch_shapes=[
            pltpu.VMEM((n_peer, toks, feats), BF16),
            pltpu.VMEM((2, n_col, 2, small, units), BF16),
            line, line, line, line, line,
            pltpu.VMEM((n_chunk, 2, 3, subtok, width), BF16),
            pltpu.VMEM((n_peer, toks, feats), F32),
            pltpu.VMEM((feats, units), BF16),
            pltpu.VMEM((feats, units), BF16),
            pltpu.VMEM((2, width, feats), BF16),
            dma((n_peer,)), dma((n_peer,)), dma((n_row,)), dma((n_row,)),
            dma((2,)), dma((2,)), dma((5,)),
            dma((2, n_col, 4)), dma((2, n_col, 4)),
            dma((2, n_chunk)), dma((2, n_chunk)),
            dma((n_chunk,)), dma((n_chunk,)), dma((n_chunk,)),
            dma((2,)), dma((2,)),
        ],
        compiler_params=pltpu.CompilerParams(
            collective_id=0, has_side_effects=True, vmem_limit_bytes=63 * 2**20
        ),
        name="exchange",
    )(x, og, g, u, gw, uw, dw)


def weight_grad_kernel(x_ref, og_ref, act_ref, gate_ref, up_ref, down_ref):
    x = x_ref[...]
    gate_ref[0] = dot_first(x, act_ref[0]).astype(BF16)
    up_ref[0] = dot_first(x, act_ref[1]).astype(BF16)
    down_ref[0] = dot_first(act_ref[2], og_ref[...]).astype(BF16)


def weight_grads(x, og, act):
    subtok, feats = x.shape
    units = act.shape[2]
    tile = 512 if units % 512 == 0 else 256
    whole = pl.BlockSpec((subtok, feats), lambda i: (0, 0))
    wide = pl.BlockSpec((1, feats, tile), lambda i: (0, 0, i))
    return pl.pallas_call(
        weight_grad_kernel,
        grid=(units // tile,),
        out_shape=(
            jax.ShapeDtypeStruct((1, feats, units), BF16),
            jax.ShapeDtypeStruct((1, feats, units), BF16),
            jax.ShapeDtypeStruct((1, units, feats), BF16),
        ),
        in_specs=[whole, whole, pl.BlockSpec((3, subtok, tile), lambda i: (0, 0, i))],
        out_specs=(wide, wide, pl.BlockSpec((1, tile, feats), lambda i: (0, i, 0))),
        compiler_params=pltpu.CompilerParams(vmem_limit_bytes=60 * 2**20),
        cost_estimate=pl.CostEstimate(
            flops=6 * subtok * feats * units,
            bytes_accessed=6 * units * (feats + subtok) + 4 * subtok * feats,
            transcendentals=0,
        ),
        name="weight_grads",
    )(x, og, act)


def solution(mesh):
    n_row, n_col = mesh.shape["row"], mesh.shape["col"]

    def at(i):
        return i % n_row * 2 + i // n_row

    def shards(x, og, g, u, gw, uw, dw):
        x_all, og_all, act, *parts = exchange(n_row, n_col, x, og, g, u, gw, uw, dw)
        feats, n_peer = x.shape[2], 2 * n_row
        arrived = [
            lax.ppermute(
                parts[k], ("row", "depth"), [(at(i), at((i + k) % n_peer)) for i in range(n_peer)]
            )
            for k in range(1, n_peer)
        ]
        grads = weight_grads(x_all.reshape(-1, feats), og_all.reshape(-1, feats), act)
        total = sum((part.astype(F32) for part in arrived), parts[0].astype(F32))
        return (total.astype(BF16)[None], *grads)

    return jax.shard_map(
        shards,
        mesh=mesh,
        in_specs=(
            P(("groups", "depth"), "row", "col"),
            P(("groups", "depth"), "row", "col"),
            P(("groups", "depth"), "col", "row"),
            P(("groups", "depth"), "col", "row"),
            P("col", ("row", "depth")),
            P("col", ("row", "depth")),
            P(("row", "depth"), "col"),
        ),
        out_specs=(
            P(("groups", "depth"), "row", "col"),
            P(("groups", "depth"), "col", "row"),
            P(("groups", "depth"), "col", "row"),
            P(("groups", "depth"), "row", "col"),
        ),
        check_vma=False,
    )
```

```python
import functools

import jax
import jax.numpy as jnp
from jax import lax
from jax.experimental import pallas as pl
from jax.experimental.pallas import tpu as pltpu
from jax.sharding import PartitionSpec as P

MESH = pl.DeviceIdType.MESH
BF16 = jnp.bfloat16
F32 = jnp.float32


def dot_last(left, right):
    return lax.dot_general(
        left, right, (((1,), (1,)), ((), ())), preferred_element_type=F32
    )


def dot_first(left, right):
    return lax.dot_general(
        left, right, (((0,), (0,)), ((), ())), preferred_element_type=F32
    )


def exchange_kernel(
    n_row, n_col, n_chunk,
    x_in, og_in, g_in, u_in, gw_in, uw_in, dw_in,
    x_out, og_out, act_out, *rest,
):
    shares = rest[: 2 * n_row]
    (
        og, gu, own, fin, bin_, fout, bout, res, acc, gw, uw, dw,
        og_send, og_recv, x_send, x_recv, dep_send, dep_recv, loc,
        gu_send, gu_recv, ar_send, ar_recv, res_send, res_recv, res_loc,
        w_sem, dw_sem,
    ) = rest[2 * n_row :]
    row, col, dep = lax.axis_index("row"), lax.axis_index("col"), lax.axis_index("depth")
    other = 1 - dep
    toks = x_in.shape[1]
    small = g_in.shape[1]
    units = gw_in.shape[1]
    width = units // n_chunk
    me = dep * n_row + row
    n_peer = 2 * n_row
    has_next = col < n_col - 1
    has_prev = col > 0

    def peer(k):
        idx = lax.rem(me + k, n_peer)
        return idx, {"row": lax.rem(idx, n_row), "depth": idx // n_row}

    def next_prev(direction):
        if direction == 0:
            return has_prev, has_next, {"col": jnp.minimum(col + 1, n_col - 1)}
        return has_next, has_prev, {"col": jnp.maximum(col - 1, 0)}

    barrier = pltpu.get_barrier_semaphore()
    for k in range(1, n_peer):
        pl.semaphore_signal(barrier, inc=1, device_id=peer(k)[1], device_id_type=MESH)
    for direction in range(2):
        _, going, to = next_prev(direction)

        @pl.when(going)
        def _():
            pl.semaphore_signal(barrier, inc=1, device_id=to, device_id_type=MESH)

    load_gw = pltpu.make_async_copy(gw_in, gw, w_sem.at[0])
    load_uw = pltpu.make_async_copy(uw_in, uw, w_sem.at[1])

    def load_dw(i):
        slot = lax.rem(i, 2)
        return pltpu.make_async_copy(
            dw_in.at[pl.ds(i * width, width)], dw.at[slot], dw_sem.at[slot]
        )

    load_dw(0).start()
    own_g = [
        pltpu.make_async_copy(
            src.at[0, :, pl.ds(pl.multiple_of(dep * units, 128), units)],
            gu.at[a, col, dep], loc.at[a],
        )
        for a, src in enumerate((g_in, u_in))
    ]
    for copy in own_g:
        copy.start()
    own_og = pltpu.make_async_copy(og_in.at[0], og.at[me], loc.at[2])
    own_og.start()
    own_x = pltpu.make_async_copy(x_in.at[0], x_out.at[row], loc.at[3])
    own_x.start()

    beside = jnp.where(has_next, 1, 0) + jnp.where(has_prev, 1, 0)
    pl.semaphore_wait(barrier, n_peer - 1 + beside)

    dep_copies = [
        pltpu.make_async_remote_copy(
            src_ref=src.at[0, :, pl.ds(pl.multiple_of(other * units, 128), units)],
            dst_ref=gu.at[a, col, dep],
            send_sem=dep_send.at[a], recv_sem=dep_recv.at[a],
            device_id={"depth": other}, device_id_type=MESH,
        )
        for a, src in enumerate((g_in, u_in))
    ]

    def arrived(a):
        return pltpu.make_async_remote_copy(
            src_ref=gu.at[a, col, other], dst_ref=gu.at[a, col, other],
            send_sem=dep_send.at[a], recv_sem=dep_recv.at[a],
            device_id={"depth": other}, device_id_type=MESH,
        )

    def og_copy(k):
        idx, to = peer(k)
        return pltpu.make_async_remote_copy(
            src_ref=og_in.at[0], dst_ref=og.at[me],
            send_sem=og_send.at[k], recv_sem=og_recv.at[me],
            device_id=to, device_id_type=MESH,
        )

    def og_from(k):
        idx, to = peer(k)
        return pltpu.make_async_remote_copy(
            src_ref=og.at[idx], dst_ref=og.at[idx],
            send_sem=og_send.at[k], recv_sem=og_recv.at[idx],
            device_id=to, device_id_type=MESH,
        )

    def x_copy(k):
        idx = lax.rem(row + k, n_row)
        return pltpu.make_async_remote_copy(
            src_ref=x_in.at[0], dst_ref=x_out.at[row],
            send_sem=x_send.at[k], recv_sem=x_recv.at[row],
            device_id={"row": idx}, device_id_type=MESH,
        )

    def x_from(k):
        idx = lax.rem(row + k, n_row)
        return pltpu.make_async_remote_copy(
            src_ref=x_out.at[idx], dst_ref=x_out.at[idx],
            send_sem=x_send.at[k], recv_sem=x_recv.at[idx],
            device_id={"row": idx}, device_id_type=MESH,
        )

    def gu_copy(direction, block, a, s):
        to = next_prev(direction)[2]
        m = 2 * a + s
        return pltpu.make_async_remote_copy(
            src_ref=gu.at[a, block, s], dst_ref=gu.at[a, block, s],
            send_sem=gu_send.at[direction, block, m],
            recv_sem=gu_recv.at[direction, block, m],
            device_id=to, device_id_type=MESH,
        )

    for copy in own_g:
        copy.wait()
    for a in range(2):
        for direction in range(2):
            @pl.when(next_prev(direction)[1])
            def _():
                gu_copy(direction, col, a, dep).start()
    for copy in dep_copies:
        copy.start()
    for k in range(1, n_peer):
        og_copy(k).start()
    for a in range(2):
        arrived(a).wait_recv()
        for direction in range(2):
            @pl.when(next_prev(direction)[1])
            def _():
                gu_copy(direction, col, a, other).start()
    for k in range(1, n_row):
        x_copy(k).start()
    load_gw.start()
    load_uw.start()

    own_og.wait()
    for k in range(1, n_peer):
        og_from(k).wait_recv()
    keep_og = pltpu.make_async_copy(og.at[pl.ds(dep * n_row, n_row)], og_out, loc.at[4])
    keep_og.start()

    def partial(i, _):
        load_dw(i).wait()

        @pl.when(i + 1 < n_chunk)
        def _():
            load_dw(i + 1).start()
        rows = og[...].reshape(n_peer * toks, og.shape[2])
        product = dot_last(rows, dw[lax.rem(i, 2)])
        own[i] = product.reshape(2 * n_col, small, width).astype(BF16)
        return 0

    lax.fori_loop(0, n_chunk, partial, 0)

    def gu_step(step):
        for m in range(4):
            a, s = m % 2, m // 2
            for direction in range(2):
                coming, going, _ = next_prev(direction)
                block = col - 1 - step if direction == 0 else col + 1 + step
                valid = (block >= 0) & (block < n_col)
                half = dep if s == 0 else other

                @pl.when(valid)
                def _():
                    gu_copy(direction, block, a, half).wait_recv()

                    @pl.when(going)
                    def _():
                        gu_copy(direction, block, a, half).start()

    def gu_sent(step):
        for m in range(4):
            for direction in range(2):
                _, going, _ = next_prev(direction)
                block = col - step if direction == 0 else col + step
                valid = (block >= 0) & (block < n_col)

                @pl.when(valid & going)
                def _():
                    gu_copy(direction, block, m // 2, m % 2).wait_send()

    def ar_copy(direction, i, src):
        dst = fin if direction == 0 else bin_
        return pltpu.make_async_remote_copy(
            src_ref=src.at[i], dst_ref=dst.at[i],
            send_sem=ar_send.at[direction, i], recv_sem=ar_recv.at[direction, i],
            device_id=next_prev(direction)[2], device_id_type=MESH,
        )

    gu_step(0)
    gu_sent(0)
    for direction in range(2):
        coming, going, _ = next_prev(direction)

        @pl.when(jnp.logical_not(coming))
        def _():
            def first(i, _):
                ar_copy(direction, i, own).start()
                return 0
            lax.fori_loop(0, n_chunk, first, 0)
            land = fin if direction == 0 else bin_

            def clear(i, _):
                land[i] = jnp.zeros(land.shape[1:], BF16)
                return 0
            lax.fori_loop(0, n_chunk, clear, 0)

    if n_col > 2:
        def later(step, _):
            gu_step(step)
            return 0
        lax.fori_loop(1, n_col - 1, later, 0)

    load_gw.wait()
    load_uw.wait()
    acc[...] = jnp.zeros_like(acc)
    half_col = n_col // 2

    def res_copy(i):
        at = pl.multiple_of(dep * units + i * width, 128)
        return pltpu.make_async_remote_copy(
            src_ref=res.at[i, other], dst_ref=act_out.at[:, :, pl.ds(at, width)],
            send_sem=res_send.at[i], recv_sem=res_recv.at[i],
            device_id={"depth": other}, device_id_type=MESH,
        )

    def res_from(i):
        at = pl.multiple_of(other * units + i * width, 128)
        there = act_out.at[:, :, pl.ds(at, width)]
        return pltpu.make_async_remote_copy(
            src_ref=there, dst_ref=there,
            send_sem=res_send.at[i], recv_sem=res_recv.at[i],
            device_id={"depth": other}, device_id_type=MESH,
        )

    def res_keep(i):
        at = pl.multiple_of(dep * units + i * width, 128)
        return pltpu.make_async_copy(
            res.at[i, dep], act_out.at[:, :, pl.ds(at, width)], res_loc.at[i]
        )

    def slot(t, _):
        for direction in range(2):
            coming, going, _ = next_prev(direction)
            hops = col if direction == 0 else n_col - 1 - col
            i = t - hops
            land, leave = ((fin, fout), (bin_, bout))[direction]

            @pl.when(coming & (i >= 0) & (i < n_chunk))
            def _():
                ar_copy(direction, i, leave).wait_recv()

                @pl.when(going)
                def _():
                    leave[i] = (land[i].astype(F32) + own[i].astype(F32)).astype(BF16)
                    ar_copy(direction, i, leave).start()

        i = t - jnp.maximum(col, n_col - 1 - col)

        @pl.when((i >= 0) & (i < n_chunk))
        def _():
            cols = pl.ds(pl.multiple_of(i * width, 128), width)
            for s in (other, dep):
                def pair(p, _):
                    blocks = pl.ds(s * n_col + 2 * p, 2)
                    pair_at = pl.ds(2 * p, 2)
                    shape = (2 * small, width)
                    hg = (
                        fin[i, blocks].astype(F32) + own[i, blocks].astype(F32)
                        + bin_[i, blocks].astype(F32)
                    ).reshape(shape)
                    gate = gu[0, pair_at, s, :, cols].astype(F32).reshape(shape)
                    up = gu[1, pair_at, s, :, cols].astype(F32).reshape(shape)
                    sig = 1.0 / (1.0 + jnp.exp(-gate))
                    silu = gate * sig
                    at = pl.ds(pl.multiple_of(p * 2 * small, 16), 2 * small)
                    res[i, s, 0, at] = (hg * up * sig * (1.0 + gate * (1.0 - sig))).astype(BF16)
                    res[i, s, 1, at] = (hg * silu).astype(BF16)
                    res[i, s, 2, at] = (silu * up).astype(BF16)
                    return 0
                lax.fori_loop(0, half_col, pair, 0)
                if s is other:
                    res_copy(i).start()
            res_keep(i).start()
            for s in range(2):
                of_sub = pl.ds(s * n_row, n_row)
                acc[of_sub] += (
                    dot_last(res[i, s, 0], gw[:, cols]) + dot_last(res[i, s, 1], uw[:, cols])
                ).reshape(n_row, toks, acc.shape[2])
        return 0

    lax.fori_loop(0, n_chunk + n_col - 1, slot, 0)

    for k in range(n_peer):
        shares[k][...] = acc[peer(k)[0]].astype(BF16)

    def finish(i, _):
        res_from(i).wait_recv()
        res_copy(i).wait_send()
        res_keep(i).wait()
        for direction in range(2):
            @pl.when(next_prev(direction)[1])
            def _():
                ar_copy(direction, i, own).wait_send()
        return 0

    lax.fori_loop(0, n_chunk, finish, 0)
    if n_col > 1:
        def sent(step, _):
            gu_sent(step)
            return 0
        lax.fori_loop(1, n_col - 1, sent, 0)
    for copy in dep_copies:
        copy.wait_send()
    own_x.wait()
    keep_og.wait()
    for k in range(1, n_row):
        x_copy(k).wait_send()
        x_from(k).wait_recv()
    for k in range(1, n_peer):
        og_copy(k).wait_send()


def exchange(n_row, n_col, x, og, g, u, gw, uw, dw):
    toks, feats = x.shape[1:]
    small = g.shape[1]
    units = gw.shape[1]
    n_chunk = 14 if units % (14 * 128) == 0 else 7
    width = units // n_chunk
    n_peer = 2 * n_row
    subtok = toks * n_row
    anywhere = pl.BlockSpec(memory_space=pl.ANY)
    line = pltpu.VMEM((n_chunk, 2 * n_col, small, width), BF16)
    dma = pltpu.SemaphoreType.DMA
    return pl.pallas_call(
        functools.partial(exchange_kernel, n_row, n_col, n_chunk),
        out_shape=(
            jax.ShapeDtypeStruct((n_row, toks, feats), BF16),
            jax.ShapeDtypeStruct((n_row, toks, feats), BF16),
            jax.ShapeDtypeStruct((3, subtok, 2 * units), BF16),
            *[jax.ShapeDtypeStruct((toks, feats), BF16)] * n_peer,
        ),
        in_specs=[anywhere] * 7,
        out_specs=(anywhere, anywhere, anywhere, *[pl.BlockSpec(memory_space=pltpu.VMEM)] * n_peer),
        scratch_shapes=[
            pltpu.VMEM((n_peer, toks, feats), BF16),
            pltpu.VMEM((2, n_col, 2, small, units), BF16),
            line, line, line, line, line,
            pltpu.VMEM((n_chunk, 2, 3, subtok, width), BF16),
            pltpu.VMEM((n_peer, toks, feats), F32),
            pltpu.VMEM((feats, units), BF16),
            pltpu.VMEM((feats, units), BF16),
            pltpu.VMEM((2, width, feats), BF16),
            dma((n_peer,)), dma((n_peer,)), dma((n_row,)), dma((n_row,)),
            dma((2,)), dma((2,)), dma((5,)),
            dma((2, n_col, 4)), dma((2, n_col, 4)),
            dma((2, n_chunk)), dma((2, n_chunk)),
            dma((n_chunk,)), dma((n_chunk,)), dma((n_chunk,)),
            dma((2,)), dma((2,)),
        ],
        compiler_params=pltpu.CompilerParams(
            collective_id=0, has_side_effects=True, vmem_limit_bytes=63 * 2**20
        ),
        name="exchange",
    )(x, og, g, u, gw, uw, dw)


def weight_grad_kernel(x_ref, og_ref, act_ref, gate_ref, up_ref, down_ref):
    x = x_ref[...]
    gate_ref[0] = dot_first(x, act_ref[0]).astype(BF16)
    up_ref[0] = dot_first(x, act_ref[1]).astype(BF16)
    down_ref[0] = dot_first(act_ref[2], og_ref[...]).astype(BF16)


def weight_grads(x, og, act):
    subtok, feats = x.shape
    units = act.shape[2]
    tile = max(t for t in range(128, 1025, 128) if units % t == 0)
    whole = pl.BlockSpec((subtok, feats), lambda i: (0, 0))
    wide = pl.BlockSpec((1, feats, tile), lambda i: (0, 0, i))
    return pl.pallas_call(
        weight_grad_kernel,
        grid=(units // tile,),
        out_shape=(
            jax.ShapeDtypeStruct((1, feats, units), BF16),
            jax.ShapeDtypeStruct((1, feats, units), BF16),
            jax.ShapeDtypeStruct((1, units, feats), BF16),
        ),
        in_specs=[whole, whole, pl.BlockSpec((3, subtok, tile), lambda i: (0, 0, i))],
        out_specs=(wide, wide, pl.BlockSpec((1, tile, feats), lambda i: (0, i, 0))),
        compiler_params=pltpu.CompilerParams(vmem_limit_bytes=60 * 2**20),
        cost_estimate=pl.CostEstimate(
            flops=6 * subtok * feats * units,
            bytes_accessed=6 * units * (feats + subtok) + 4 * subtok * feats,
            transcendentals=0,
        ),
        name="weight_grads",
    )(x, og, act)


def solution(mesh):
    n_row, n_col = mesh.shape["row"], mesh.shape["col"]

    def at(i):
        return i % n_row * 2 + i // n_row

    def shards(x, og, g, u, gw, uw, dw):
        x_all, og_all, act, *parts = exchange(n_row, n_col, x, og, g, u, gw, uw, dw)
        feats, n_peer = x.shape[2], 2 * n_row
        arrived = [
            lax.ppermute(
                parts[k], ("row", "depth"), [(at(i), at((i + k) % n_peer)) for i in range(n_peer)]
            )
            for k in range(1, n_peer)
        ]
        grads = weight_grads(x_all.reshape(-1, feats), og_all.reshape(-1, feats), act)
        total = sum((part.astype(F32) for part in arrived), parts[0].astype(F32))
        return (total.astype(BF16)[None], *grads)

    return jax.shard_map(
        shards,
        mesh=mesh,
        in_specs=(
            P(("groups", "depth"), "row", "col"),
            P(("groups", "depth"), "row", "col"),
            P(("groups", "depth"), "col", "row"),
            P(("groups", "depth"), "col", "row"),
            P("col", ("row", "depth")),
            P("col", ("row", "depth")),
            P(("row", "depth"), "col"),
        ),
        out_specs=(
            P(("groups", "depth"), "row", "col"),
            P(("groups", "depth"), "col", "row"),
            P(("groups", "depth"), "col", "row"),
            P(("groups", "depth"), "row", "col"),
        ),
        check_vma=False,
    )
```
